32 devices in a mesh: groups: 2 (over x), right: 4 (over y, core), left: 4 (over z).
Axes of the slice: x: 2, y: 2, z: 4, core: 2. Of those that a mesh axis runs over, the one named last changes fastest.
Arguments:
- left_act: bfloat16 [4096, 8192], P(('groups', 'right'), 'left'), parts along dimension 0, may hold values from -15 to 15
- right_act: bfloat16 [4096, 4096], P(('groups', 'left'), 'right'), parts along dimension 0, may hold values from -15 to 15
- counts: int32 [512, 128], P(('groups', 'left'), 'right'), parts along dimension 0, may hold values from 512 to 2048
- w_out: bfloat16 [1024, 128], replicated, may hold values from -0.1875 to 0.1875
Outputs:
- pair_update: float32 [512, 128, 128], P(('groups', 'left'), 'right'), parts along dimension 0
The draws below stay inside these ranges and needn't reach their ends.
There are 2 independent parts, one for each index of `groups`. The reference program is written for one: setup_inputs(seed, part) draws one part's arguments, and reference() takes and returns one part's arrays. A program takes and returns all parts, laid end to end along the dimension named above; an argument that names none is the same for every part. Nothing has to cross between parts.
All inputs are finite; a program needn't handle non-finite values.
Results may differ from the reference program's by a relative error of at most 0.0029.
Values may be sent and summed in bfloat16 or wider, within the bound.
No kernel may reach another device: no remote copies, remote signals or barrier semaphores. Data moves between devices by JAX's collectives and lax.ppermute only.
A program may use at most 128 MiB of HBM per device.

```python
import jax
import jax.numpy as jnp
from jax import lax

CH = 32
PAIR = 128
SEQS = 2048
LEFT = 256
RIGHT = 128


def place_ends(array, key, smallest, top_value):
    longest = array.shape.index(max(array.shape))
    spots = []
    for shift in (0, 1):
        where = [jax.random.randint(jax.random.fold_in(key, axis), (), 0, length) for axis, length in enumerate(array.shape)]
        where[longest] = (where[longest] + shift) % array.shape[longest]
        spots.append(tuple(where))
    return array.at[spots[0]].set(smallest).at[spots[1]].set(top_value)


def shard_levels(key, dims, pieces, least, largest):
    level, own = 1.0, jax.random.fold_in(key, 6)
    for position, shards_of in pieces:
        heights = jnp.exp(jax.random.uniform(jax.random.fold_in(own, position), (shards_of,), jnp.float32, least / len(pieces), largest / len(pieces)))
        level = level * jnp.repeat(heights, dims[position] // shards_of).reshape([-1 if axis == position else 1 for axis in range(len(dims))])
    return level


def bell_draw(rng, dims, spread, most, split=(), kind=jnp.bfloat16):
    values = jax.random.normal(rng, dims, jnp.float32) * spread
    if len(split) > 0:
        values = shard_levels(rng, dims, split, -0.22, 0.18) * values
    return jnp.clip(values, min=-most, max=most).astype(kind)


def setup_inputs(seed: int = 0, part: int = 0) -> dict:
    splits = jax.random.split(jax.random.key(seed), 5)
    own_keys = jax.random.split(jax.random.fold_in(splits[4], part), 5)
    left_act = bell_draw(own_keys[0], (SEQS, LEFT * CH), 3.0, 15.0, ((0, 4), (1, 4)))
    right_act = bell_draw(own_keys[1], (SEQS, RIGHT * CH), 3.0, 15.0, ((0, 4), (1, 4)))
    counts = place_ends(jax.random.randint(own_keys[2], (LEFT, RIGHT), SEQS // 4, SEQS + 1), jax.random.fold_in(own_keys[2], 1), SEQS // 4, SEQS).astype(jnp.int32)
    w_out = bell_draw(splits[3], (CH * CH, PAIR), (CH * CH) ** -0.5, 0.1875)
    return dict(left_act=left_act, right_act=right_act, counts=counts, w_out=w_out)


def reference(left_act, right_act, counts, w_out):
    block = 16 if LEFT % 16 == 0 else 2
    width = block * CH

    def one_block(index):
        columns = lax.dynamic_slice_in_dim(left_act, (index * width).astype(jnp.int32), width, 1)
        outer = lax.dot_general(columns, right_act, (((0,), (0,)), ((), ())), preferred_element_type=jnp.float32)
        outer = outer.reshape(block, CH, RIGHT, CH).transpose(0, 2, 1, 3).reshape(block * RIGHT, CH * CH)
        flat = outer.astype(jnp.bfloat16)
        projected = jnp.dot(flat, w_out, preferred_element_type=jnp.float32).reshape(block, RIGHT, PAIR)
        cover = lax.dynamic_slice_in_dim(counts, (index * block).astype(jnp.int32), block, 0)
        return projected / cover.astype(jnp.float32)[:, :, None]

    blocks = lax.map(one_block, jnp.arange(LEFT // block, dtype=jnp.int32))
    return blocks.reshape(LEFT, RIGHT, PAIR)
```

```python
import functools

import jax
import jax.numpy as jnp
from jax import lax
from jax.experimental import pallas as pl
from jax.experimental.pallas import tpu as pltpu
from jax.sharding import PartitionSpec as P

CH = 32
LANES = 128
GROUP = LANES // CH
CORES = 2
PARTS = 2


def spread_weights(w_out):
    pair = w_out.shape[1]
    by_e = w_out.reshape(CH, CH, pair).transpose(1, 0, 2)
    same = jnp.eye(GROUP, dtype=jnp.bool_)[None, :, None, :, None]
    full = jnp.where(same, by_e[:, None, :, None, :], jnp.zeros((), w_out.dtype))
    return full.reshape(CH * LANES, GROUP * pair)


def kernel(line, nl, nr, part, *refs):
    left_refs, right_refs = refs[:nl], refs[nl : nl + nr]
    wide_ref, counts_ref = refs[nl + nr : nl + nr + 2]
    out_ref, left_v, right_v, rt, lhs, wide_v, counts_v, out_v, left_sem, right_sem, misc_sem = refs[-11:]
    seqs, width = left_v.shape
    cols = right_v.shape[1]
    res = cols // CH
    lrows = left_refs[0].shape[0]
    rrows = right_refs[0].shape[0]
    if line:
        l, r = lax.axis_index("left"), lax.axis_index("right")
        low = l < 2
        end = jnp.logical_or(l == 0, l == 3)

        def slot(s):
            return jnp.where(s // 2 == l // 2, (s + l) % 2, jnp.where(low, s, 3 - s))

        flip = r % 2
        near = r + 1 - 2 * flip
        far = (r + 2) % 4
        owners = (r, near, far, far + 1 - 2 * flip)
        places = [slot(s) for s in owners]
    else:
        places = [0]

    for b, place in enumerate(places):
        pltpu.make_async_copy(
            left_refs[b], left_v.at[pl.ds(pl.multiple_of(place * lrows, lrows), lrows), :], left_sem.at[b]
        ).start()

    def right_copy(src, b):
        return pltpu.make_async_copy(src, right_v.at[pl.ds(b * rrows, rrows), :], right_sem.at[b])

    if line:
        own, first, mid_a, end_a, mid_b, end_b = right_refs
        right_copy(own, 0).start()
        right_copy(first, 1).start()
        for b, at_mid, at_end in ((2, mid_a, end_a), (3, mid_b, end_b)):

            @pl.when(end)
            def _():
                right_copy(at_end, b).start()

            @pl.when(jnp.logical_not(end))
            def _():
                right_copy(at_mid, b).start()
    else:
        right_copy(right_refs[0], 0).start()
    wide_copy = pltpu.make_async_copy(wide_ref, wide_v, misc_sem.at[0])
    wide_copy.start()
    counts_copy = pltpu.make_async_copy(counts_ref, counts_v, misc_sem.at[1])
    counts_copy.start()

    to = lax.broadcasted_iota(jnp.int32, (cols, cols), 0)
    source = lax.broadcasted_iota(jnp.int32, (cols, cols), 1)
    perm = jnp.where(source == (to % res) * CH + to // res, 1.0, 0.0).astype(jnp.bfloat16)
    for b in range(seqs // rrows):
        right_copy(right_refs[0], b).wait()
        rows = pl.ds(b * rrows, rrows)
        rt[:, rows] = lax.dot_general(
            perm, right_v[rows, :], (((1,), (1,)), ((), ())), preferred_element_type=jnp.float32
        ).astype(jnp.bfloat16)
    for b in range(nl):
        pltpu.make_async_copy(left_refs[b], left_v.at[pl.ds(b * lrows, lrows), :], left_sem.at[b]).wait()
    outer = jnp.dot(rt[...], left_v[...], preferred_element_type=jnp.float32).astype(jnp.bfloat16)
    for g in range(width // LANES):
        for e in range(CH):
            lhs[g * res : (g + 1) * res, e * LANES : (e + 1) * LANES] = outer[
                e * res : (e + 1) * res, g * LANES : (g + 1) * LANES
            ]
    wide_copy.wait()
    counts_copy.wait()
    projected = jnp.dot(lhs[...], wide_v[...], preferred_element_type=jnp.float32)
    pair = out_v.shape[2]
    for g in range(width // LANES):
        for i in range(GROUP):
            row = g * GROUP + i
            out_v[row] = projected[g * res : (g + 1) * res, i * pair : (i + 1) * pair] / counts_v[:, row : row + 1]
    out_copy = pltpu.make_async_copy(out_v, out_ref.at[:, pl.ds(part * res, res), :], misc_sem.at[2])
    out_copy.start()
    out_copy.wait()


def pair_features(line, part, lefts, rights, wide, counts, right_dev, before):
    nl, nr = len(lefts), len(rights)
    seqs = lefts[0].shape[0] * nl
    width = lefts[0].shape[1]
    cols = rights[0].shape[1]
    res, left_dev = cols // CH, width // CH
    pair = wide.shape[1] // GROUP
    any_space = pl.BlockSpec(memory_space=pl.ANY)
    operands = [*lefts, *rights, wide, counts]
    aliases = {}
    if before is not None:
        aliases = {len(operands): 0}
        operands.append(before)
    return pl.pallas_call(
        functools.partial(kernel, line, nl, nr, part),
        out_shape=jax.ShapeDtypeStruct((left_dev, right_dev, pair), jnp.float32),
        in_specs=[any_space] * len(operands),
        out_specs=any_space,
        input_output_aliases=aliases,
        scratch_shapes=[
            pltpu.VMEM((seqs, width), jnp.bfloat16),
            pltpu.VMEM((seqs, cols), jnp.bfloat16),
            pltpu.VMEM((cols, seqs), jnp.bfloat16),
            pltpu.VMEM((width // LANES * res, CH * LANES), jnp.bfloat16),
            pltpu.VMEM(wide.shape, jnp.bfloat16),
            pltpu.VMEM(counts.shape, jnp.float32),
            pltpu.VMEM((left_dev, res, pair), jnp.float32),
            pltpu.SemaphoreType.DMA((nl,)),
            pltpu.SemaphoreType.DMA((4,)),
            pltpu.SemaphoreType.DMA((3,)),
        ],
        compiler_params=pltpu.CompilerParams(vmem_limit_bytes=48 * 2**20),
        cost_estimate=pl.CostEstimate(
            flops=2 * seqs * width * cols, bytes_accessed=2 * seqs * (width + cols), transcendentals=0
        ),
    )(*operands)


def tied(*values):
    return lax.optimization_barrier(values)


def gather_line(left_act, right_act):
    ends = ((0, 1), (1, 0), (2, 3), (3, 2))
    middle = ((1, 2), (2, 1))
    outward = ((1, 0), (2, 3))

    def hop(x, pairs):
        return lax.ppermute(x, "left", pairs)

    def partner(x, step):
        return lax.ppermute(x, "right", [(i, i ^ step) for i in range(4)])

    a, c = jnp.split(right_act, PARTS, axis=1)
    a1, a2 = hop(a, ends), hop(a, middle)
    far = partner(left_act, CORES)
    near = partner(left_act, 1)
    c1, c2 = hop(c, ends), hop(c, middle)
    a1, a2 = tied(a1, a2)
    a3, a4 = hop(a2, outward), hop(a1, middle)
    c1, c2 = tied(c1, c2)
    c3, c4 = hop(c2, outward), hop(c1, middle)
    a3, a4 = tied(a3, a4)
    a5 = hop(a4, outward)
    c3, c4 = tied(c3, c4)
    c5 = hop(c4, outward)
    cross = partner(far, 1)
    return [left_act, near, far, cross], [(a, a1, a2, a3, a4, a5), (c, c1, c2, c3, c4, c5)]


def shards(line, left_act, right_act, counts, w_out):
    if line:
        lefts, rights = gather_line(left_act, right_act)
    else:
        lefts = [lax.all_gather(left_act, "right", axis=0, tiled=True)]
        full = lax.all_gather(right_act, "left", axis=0, tiled=True)
        rights = [(x,) for x in jnp.split(full, PARTS, axis=1)]
    wide = spread_weights(w_out)
    by_right = jnp.split(counts.astype(jnp.float32).T, PARTS, axis=0)
    out = None
    for part in range(PARTS):
        out = pair_features(line, part, lefts, rights[part], wide, by_right[part], counts.shape[1], out)
    return out


def solution(mesh):
    in_specs = (
        P(("groups", "right"), "left"),
        P(("groups", "left"), "right"),
        P(("groups", "left"), "right"),
        P(),
    )
    out_specs = P(("groups", "left"), "right", None)
    line = mesh.shape["left"] == 4 and mesh.shape["right"] == 4
    body = functools.partial(shards, line)
    return jax.shard_map(body, mesh=mesh, in_specs=in_specs, out_specs=out_specs, check_vma=False)
```

```python
import functools

import jax
import jax.numpy as jnp
from jax import lax
from jax.experimental import pallas as pl
from jax.experimental.pallas import tpu as pltpu
from jax.sharding import PartitionSpec as P

CH = 32
LANES = 128
GROUP = LANES // CH
CORES = 2
FIRST_PART, PART_UNITS = 1, 2
LEFT_PARTS = 4
EARLY_VMEM = 40 * 2**20
LATE_VMEM = 24 * 2**20


def spread_weights(w_out):
    pair = w_out.shape[1]
    by_e = w_out.reshape(CH, CH, pair).transpose(1, 0, 2)
    same = jnp.eye(GROUP, dtype=jnp.bool_)[None, :, None, :, None]
    full = jnp.where(same, by_e[:, None, :, None, :], jnp.zeros((), w_out.dtype))
    return full.reshape(CH * LANES, GROUP * pair)


def turned(right, perm):
    return lax.dot_general(perm, right, (((1,), (1,)), ((), ())), preferred_element_type=jnp.float32).astype(
        jnp.bfloat16
    )


def regroup(cols):
    res = cols // CH
    to = lax.broadcasted_iota(jnp.int32, (cols, cols), 0)
    source = lax.broadcasted_iota(jnp.int32, (cols, cols), 1)
    return jnp.where(source == (to % res) * CH + to // res, 1.0, 0.0).astype(jnp.bfloat16)


def early_kernel(places, *refs):
    nl = len(places)
    parts = (len(refs) - nl - 4) // 5
    lefts = refs[:nl]
    rights = refs[nl : nl + 4 * parts]
    sums = refs[nl + 4 * parts : nl + 5 * parts]
    late_ref, left_v, rt, sem = refs[nl + 5 * parts :]
    l, r = lax.axis_index("left"), lax.axis_index("right")
    end = jnp.logical_or(l == 0, l == 3)
    rows = left_v.shape[0] // 3
    flip = 1 - 2 * (r % 2)
    far = (r + 2) % 4
    owners = (r, r + flip, far, far + flip)

    copies = []
    for n, (k, col) in enumerate(places):
        s = owners[k]
        slot = jnp.where(s // 2 == l // 2, (s + l) % 2, jnp.where(l < 2, s, 3 - s))
        at = pl.multiple_of(jnp.minimum(slot, 2) * rows, rows)
        cols = pl.ds(col, lefts[n].shape[1])

        @pl.when(slot < 3)
        def _():
            pltpu.make_async_copy(lefts[n], left_v.at[pl.ds(at, rows), cols], sem.at[n]).start()

        @pl.when(slot == 3)
        def _():
            pltpu.make_async_copy(lefts[n], late_ref.at[:, cols], sem.at[n]).start()

        copies.append(pltpu.make_async_copy(lefts[n], late_ref.at[:, cols], sem.at[n]))

    first_row = 0
    for p in range(parts):
        own, first, mid, outer_end = rights[4 * p : 4 * p + 4]
        cols = own.shape[1]
        perm = regroup(cols)
        here = pl.ds(first_row, cols)
        rt[here, :rows] = turned(own[...], perm)
        rt[here, rows : 2 * rows] = turned(first[...], perm)

        @pl.when(end)
        def _():
            rt[here, 2 * rows :] = turned(outer_end[...], perm)

        @pl.when(jnp.logical_not(end))
        def _():
            rt[here, 2 * rows :] = turned(mid[...], perm)

        first_row += cols
    for copy in copies:
        copy.wait()
    first_row = 0
    for p in range(parts):
        cols = sums[p].shape[0]
        sums[p][...] = jnp.dot(rt[first_row : first_row + cols, :], left_v[...], preferred_element_type=jnp.float32)
        first_row += cols


def early_sums(places, lefts, rights):
    rows, width = lefts[0].shape
    vmem = pl.BlockSpec(memory_space=pltpu.VMEM)
    anywhere = pl.BlockSpec(memory_space=pl.ANY)
    parts = len(rights)
    cols = [part[0].shape[1] for part in rights]
    out = pl.pallas_call(
        functools.partial(early_kernel, places),
        out_shape=[jax.ShapeDtypeStruct((c, width), jnp.float32) for c in cols]
        + [jax.ShapeDtypeStruct((rows, width), jnp.bfloat16)],
        in_specs=[anywhere] * len(lefts) + [vmem] * (4 * parts),
        out_specs=[vmem] * parts + [anywhere],
        scratch_shapes=[
            pltpu.VMEM((3 * rows, width), jnp.bfloat16),
            pltpu.VMEM((sum(cols), 3 * rows), jnp.bfloat16),
            pltpu.SemaphoreType.DMA((len(lefts),)),
        ],
        compiler_params=pltpu.CompilerParams(vmem_limit_bytes=EARLY_VMEM),
        cost_estimate=pl.CostEstimate(flops=1, bytes_accessed=1, transcendentals=0),
    )(*lefts, *[x for part in rights for x in part])
    return out[:parts], out[parts]


def late_kernel(line, start, *refs):
    if line:
        sums, left, mid, outer_end, wide, counts = refs[:6]
    else:
        left, mid, wide, counts = refs[:4]
    out_ref, rt, lhs, out_v, sem = refs[-5:]
    cols, rows = rt.shape
    width = left.shape[1]
    res = cols // CH
    perm = regroup(cols)
    if line:
        l = lax.axis_index("left")
        end = jnp.logical_or(l == 0, l == 3)

        @pl.when(end)
        def _():
            rt[...] = turned(outer_end[...], perm)

        @pl.when(jnp.logical_not(end))
        def _():
            rt[...] = turned(mid[...], perm)

    else:
        rt[...] = turned(mid[...], perm)
    total = jnp.dot(rt[...], left[...], preferred_element_type=jnp.float32)
    if line:
        total += sums[...]
    outer = total.astype(jnp.bfloat16)
    for g in range(width // LANES):
        for e in range(CH):
            lhs[g * res : (g + 1) * res, e * LANES : (e + 1) * LANES] = outer[
                e * res : (e + 1) * res, g * LANES : (g + 1) * LANES
            ]
    projected = jnp.dot(lhs[...], wide[...], preferred_element_type=jnp.float32)
    pair = out_v.shape[2]
    for g in range(width // LANES):
        for i in range(GROUP):
            row = g * GROUP + i
            out_v[row] = projected[g * res : (g + 1) * res, i * pair : (i + 1) * pair] / counts[:, row : row + 1]
    out_copy = pltpu.make_async_copy(out_v, out_ref.at[:, pl.ds(start, res), :], sem)
    out_copy.start()
    out_copy.wait()


def pair_features(line, start, operands, counts, right_dev, before):
    vmem = pl.BlockSpec(memory_space=pltpu.VMEM)
    anywhere = pl.BlockSpec(memory_space=pl.ANY)
    left, right, wide = (operands[1], operands[2], operands[4]) if line else operands
    rows, width = left.shape
    cols = right.shape[1]
    res, left_dev = cols // CH, width // CH
    pair = wide.shape[1] // GROUP
    operands = [*operands, counts]
    specs = [vmem] * len(operands)
    aliases = {}
    if before is not None:
        aliases = {len(operands): 0}
        operands.append(before)
        specs.append(anywhere)
    return pl.pallas_call(
        functools.partial(late_kernel, line, start),
        out_shape=jax.ShapeDtypeStruct((left_dev, right_dev, pair), jnp.float32),
        in_specs=specs,
        out_specs=anywhere,
        input_output_aliases=aliases,
        scratch_shapes=[
            pltpu.VMEM((cols, rows), jnp.bfloat16),
            pltpu.VMEM((width // LANES * res, CH * LANES), jnp.bfloat16),
            pltpu.VMEM((left_dev, res, pair), jnp.float32),
            pltpu.SemaphoreType.DMA,
        ],
        compiler_params=pltpu.CompilerParams(vmem_limit_bytes=LATE_VMEM if line else 2 * LATE_VMEM),
        cost_estimate=pl.CostEstimate(flops=1, bytes_accessed=1, transcendentals=0),
    )(*operands)


def tied(*values):
    return lax.optimization_barrier(values)


def gather_line(left_act, right_act):
    ends = ((0, 1), (1, 0), (2, 3), (3, 2))
    middle = ((1, 2), (2, 1))
    outward = ((1, 0), (2, 3))

    def hop(x, pairs):
        return lax.ppermute(x, "left", pairs)

    def partner(x, step):
        return lax.ppermute(x, "right", [(i, i ^ step) for i in range(4)])

    cut = right_act.shape[1] * FIRST_PART // PART_UNITS
    a, c = right_act[:, :cut], right_act[:, cut:]
    width = left_act.shape[1] // LEFT_PARTS
    quarters = [left_act[:, n * width : (n + 1) * width] for n in range(LEFT_PARTS)]
    near = partner(left_act, 1)
    a1, a2, far0 = hop(a, ends), hop(a, middle), partner(quarters[0], CORES)
    c1, c2, far1 = hop(c, ends), hop(c, middle), partner(quarters[1], CORES)
    a1, a2, far0, quarters[2] = tied(a1, a2, far0, quarters[2])
    a3, a4, far2 = hop(a2, outward), hop(a1, middle), partner(quarters[2], CORES)
    c1, c2, far1, quarters[3] = tied(c1, c2, far1, quarters[3])
    c3, c4, far3 = hop(c2, outward), hop(c1, middle), partner(quarters[3], CORES)
    a3, a4, far2 = tied(a3, a4, far2)
    a5 = hop(a4, outward)
    cross = [partner(x, 1) for x in (far0, far2)]
    c3, c4, far3 = tied(c3, c4, far3)
    c5 = hop(c4, outward)
    cross += [partner(x, 1) for x in (far1, far3)]
    lefts = [left_act, near, far0, far2, far1, far3, *cross]
    order = [0, 2, 1, 3]
    places = [(0, 0), (1, 0)] + [(2, n * width) for n in order] + [(3, n * width) for n in order]
    return places, lefts, ((a, a1, a2, a3), (c, c1, c2, c3)), ((a4, a5), (c4, c5))


def shards(line, left_act, right_act, counts, w_out):
    right_dev = counts.shape[1]
    cut = right_dev * FIRST_PART // PART_UNITS
    by_right = counts.astype(jnp.float32).T
    count_parts = (by_right[:cut], by_right[cut:])
    wide = spread_weights(w_out)
    if line:
        places, lefts, early, late = gather_line(left_act, right_act)
        sums, left_late = early_sums(places, lefts, early)
        operands = [(sums[p], left_late, *late[p], wide) for p in range(2)]
    else:
        left_full = lax.all_gather(left_act, "right", axis=0, tiled=True)
        full = lax.all_gather(right_act, "left", axis=0, tiled=True)
        operands = [(left_full, x, wide) for x in (full[:, : cut * CH], full[:, cut * CH :])]
    out = None
    for start, given, count in zip((0, cut), operands, count_parts):
        out = pair_features(line, start, given, count, right_dev, out)
    return out


def solution(mesh):
    in_specs = (
        P(("groups", "right"), "left"),
        P(("groups", "left"), "right"),
        P(("groups", "left"), "right"),
        P(),
    )
    out_specs = P(("groups", "left"), "right", None)
    line = mesh.shape["left"] == 4 and mesh.shape["right"] == 4
    body = functools.partial(shards, line)
    return jax.shard_map(body, mesh=mesh, in_specs=in_specs, out_specs=out_specs, check_vma=False)
```

```python
import functools
import math

import jax
import jax.numpy as jnp
from jax import lax
from jax.experimental import pallas as pl
from jax.experimental.pallas import tpu as pltpu
from jax.sharding import PartitionSpec as P

CH = 32
LANES = 128
GROUP = LANES // CH
CORES = 2
FIRST_PART, PART_UNITS = 1, 2
CROSS_PARTS = (4, 3, 1)
EARLY_VMEM = 28 * 2**20
LATE_VMEM = 16 * 2**20


def spread_weights(w_out):
    pair = w_out.shape[1]
    by_e = w_out.reshape(CH, CH, pair).transpose(1, 0, 2)
    same = jnp.eye(GROUP, dtype=jnp.bool_)[None, :, None, :, None]
    full = jnp.where(same, by_e[:, None, :, None, :], jnp.zeros((), w_out.dtype))
    return full.reshape(CH * LANES, GROUP * pair)


def turned(right, perm):
    return lax.dot_general(perm, right, (((1,), (1,)), ((), ())), preferred_element_type=jnp.float32).astype(
        jnp.bfloat16
    )


def regroup(cols):
    res = cols // CH
    to = lax.broadcasted_iota(jnp.int32, (cols, cols), 0)
    source = lax.broadcasted_iota(jnp.int32, (cols, cols), 1)
    return jnp.where(source == (to % res) * CH + to // res, 1.0, 0.0).astype(jnp.bfloat16)


def early_kernel(places, *refs):
    nl = len(places)
    lefts = refs[:nl]
    own, beside, middle, opposite = refs[nl : nl + 4]
    sums = refs[nl + 4 : -4]
    late_ref, left_v, rt, sem = refs[-4:]
    l, r = lax.axis_index("left"), lax.axis_index("right")
    end = jnp.logical_or(l == 0, l == 3)
    rows = left_v.shape[0] // 3
    flip = 1 - 2 * (r % 2)
    far = (r + 2) % 4
    owners = (r, r + flip, far, far + flip)

    copies = []
    for n, (k, row) in enumerate(places):
        s = owners[k]
        odd = (s + l) % 2
        slot = jnp.where(s // 2 == l // 2, odd, 3 - odd)
        height = lefts[n].shape[0]
        at = pl.multiple_of(jnp.minimum(slot, 2) * rows + row, math.gcd(rows, row))
        late = late_ref.at[row : row + height, :]

        @pl.when(slot < 3)
        def _():
            pltpu.make_async_copy(lefts[n], left_v.at[pl.ds(at, height), :], sem.at[n]).start()

        @pl.when(slot == 3)
        def _():
            pltpu.make_async_copy(lefts[n], late, sem.at[n]).start()

        copies.append(pltpu.make_async_copy(lefts[n], late, sem.at[n]))

    first_row = 0
    for total in sums:
        cols = total.shape[0]
        perm = regroup(cols)
        here = pl.ds(first_row, cols)
        rt[here, :rows] = turned(own[:, here], perm)
        rt[here, rows : 2 * rows] = turned(beside[:, here], perm)

        @pl.when(end)
        def _():
            rt[here, 2 * rows :] = turned(opposite[:, here], perm)

        @pl.when(jnp.logical_not(end))
        def _():
            rt[here, 2 * rows :] = turned(middle[:, here], perm)

        first_row += cols
    for copy in copies:
        copy.wait()
    first_row = 0
    for total in sums:
        cols = total.shape[0]
        total[...] = jnp.dot(rt[first_row : first_row + cols, :], left_v[...], preferred_element_type=jnp.float32)
        first_row += cols


def early_sums(places, lefts, rights, cols):
    rows, width = lefts[0].shape
    vmem = pl.BlockSpec(memory_space=pltpu.VMEM)
    anywhere = pl.BlockSpec(memory_space=pl.ANY)
    parts = len(cols)
    out = pl.pallas_call(
        functools.partial(early_kernel, places),
        out_shape=[jax.ShapeDtypeStruct((c, width), jnp.float32) for c in cols]
        + [jax.ShapeDtypeStruct((rows, width), jnp.bfloat16)],
        in_specs=[anywhere] * len(lefts) + [vmem] * 4,
        out_specs=[vmem] * parts + [anywhere],
        scratch_shapes=[
            pltpu.VMEM((3 * rows, width), jnp.bfloat16),
            pltpu.VMEM((sum(cols), 3 * rows), jnp.bfloat16),
            pltpu.SemaphoreType.DMA((len(lefts),)),
        ],
        compiler_params=pltpu.CompilerParams(vmem_limit_bytes=EARLY_VMEM),
        cost_estimate=pl.CostEstimate(flops=1, bytes_accessed=1, transcendentals=0),
    )(*lefts, *rights)
    return out[:parts], out[parts]


def late_kernel(line, start, *refs):
    if line:
        sums, left, right, wide, counts = refs[:5]
    else:
        left, right, wide, counts = refs[:4]
    out_ref, rt, lhs, out_v, sem = refs[-5:]
    width = left.shape[1]
    res = right.shape[1] // CH
    rt[...] = turned(right[...], regroup(right.shape[1]))
    total = jnp.dot(rt[...], left[...], preferred_element_type=jnp.float32)
    if line:
        total += sums[...]
    outer = total.astype(jnp.bfloat16)
    for g in range(width // LANES):
        for e in range(CH):
            lhs[g * res : (g + 1) * res, e * LANES : (e + 1) * LANES] = outer[
                e * res : (e + 1) * res, g * LANES : (g + 1) * LANES
            ]
    projected = jnp.dot(lhs[...], wide[...], preferred_element_type=jnp.float32)
    pair = out_v.shape[2]
    for g in range(width // LANES):
        for i in range(GROUP):
            row = g * GROUP + i
            out_v[row] = projected[g * res : (g + 1) * res, i * pair : (i + 1) * pair] / counts[:, row : row + 1]
    out_copy = pltpu.make_async_copy(out_v, out_ref.at[:, pl.ds(start, res), :], sem)
    out_copy.start()
    out_copy.wait()


def pair_features(line, start, operands, counts, right_dev, before):
    vmem = pl.BlockSpec(memory_space=pltpu.VMEM)
    anywhere = pl.BlockSpec(memory_space=pl.ANY)
    left, right, wide = operands[-3:]
    rows, width = left.shape
    cols = right.shape[1]
    res, left_dev = cols // CH, width // CH
    pair = wide.shape[1] // GROUP
    operands = [*operands, counts]
    specs = [vmem] * len(operands)
    aliases = {}
    if before is not None:
        aliases = {len(operands): 0}
        operands.append(before)
        specs.append(anywhere)
    return pl.pallas_call(
        functools.partial(late_kernel, line, start),
        out_shape=jax.ShapeDtypeStruct((left_dev, right_dev, pair), jnp.float32),
        in_specs=specs,
        out_specs=anywhere,
        input_output_aliases=aliases,
        scratch_shapes=[
            pltpu.VMEM((cols, rows), jnp.bfloat16),
            pltpu.VMEM((width // LANES * res, CH * LANES), jnp.bfloat16),
            pltpu.VMEM((left_dev, res, pair), jnp.float32),
            pltpu.SemaphoreType.DMA,
        ],
        compiler_params=pltpu.CompilerParams(vmem_limit_bytes=LATE_VMEM if line else 2 * LATE_VMEM),
        cost_estimate=pl.CostEstimate(flops=1, bytes_accessed=1, transcendentals=0),
    )(*operands)


def gather_line(left_act, right_act, wide):
    cut = right_act.shape[1] * FIRST_PART // PART_UNITS
    end = lax.axis_index("left") % 3 == 0

    def hop(x, pairs):
        return lax.ppermute(x, "left", pairs)

    def partner(x, step):
        return lax.ppermute(x, "right", [(i, i ^ step) for i in range(4)])

    def last(cols, *arrived):
        inward = end
        for x in arrived:
            same = x[: right_act.shape[0], : cut]
            inward = jnp.logical_and(inward, same == same)
        return hop(jnp.where(inward, right_act[:, cols], middle[:, cols]), ((0, 2), (3, 1), (1, 0), (2, 3)))

    far = partner(left_act, CORES)
    near = partner(left_act, 1)
    beside = hop(right_act, [(i, i ^ 1) for i in range(4)])
    middle = hop(right_act, ((1, 2), (2, 1)))
    opposite = hop(right_act, ((0, 3), (3, 0)))
    late = (last(slice(0, cut), near, beside), last(slice(cut, None), wide))
    unit = far.shape[0] // sum(CROSS_PARTS)
    starts = [sum(CROSS_PARTS[:n]) * unit for n in range(len(CROSS_PARTS))]
    cross = [partner(far[n : n + h * unit], 1) for n, h in zip(starts, CROSS_PARTS)]
    lefts = [left_act, near, far, *cross]
    places = [(0, 0), (1, 0), (2, 0)] + [(3, n) for n in starts]
    return places, lefts, (right_act, beside, middle, opposite), late


def shards(line, left_act, right_act, counts, w_out):
    right_dev = counts.shape[1]
    cut = right_dev * FIRST_PART // PART_UNITS
    by_right = counts.astype(jnp.float32).T
    count_parts = (by_right[:cut], by_right[cut:])
    wide = spread_weights(w_out)
    if line:
        places, lefts, early, late = gather_line(left_act, right_act, wide)
        sums, left_late = early_sums(places, lefts, early, [x.shape[1] for x in late])
        operands = [(sums[p], left_late, late[p], wide) for p in range(2)]
    else:
        left_full = lax.all_gather(left_act, "right", axis=0, tiled=True)
        full = lax.all_gather(right_act, "left", axis=0, tiled=True)
        operands = [(left_full, x, wide) for x in (full[:, : cut * CH], full[:, cut * CH :])]
    out = None
    for start, given, count in zip((0, cut), operands, count_parts):
        out = pair_features(line, start, given, count, right_dev, out)
    return out


def solution(mesh):
    in_specs = (
        P(("groups", "right"), "left"),
        P(("groups", "left"), "right"),
        P(("groups", "left"), "right"),
        P(),
    )
    out_specs = P(("groups", "left"), "right", None)
    line = mesh.shape["left"] == 4 and mesh.shape["right"] == 4
    body = functools.partial(shards, line)
    return jax.shard_map(body, mesh=mesh, in_specs=in_specs, out_specs=out_specs, check_vma=False)
```

```python
import functools
import math

import jax
import jax.numpy as jnp
from jax import lax
from jax.experimental import pallas as pl
from jax.experimental.pallas import tpu as pltpu
from jax.sharding import PartitionSpec as P

CH = 32
LANES = 128
GROUP = LANES // CH
CORES = 2
FIRST_PART, PART_UNITS = 1, 2
CROSS_PARTS = (4, 3, 1)
EARLY_VMEM = 28 * 2**20
LATE_VMEM = 16 * 2**20


def spread_weights(w_out):
    pair = w_out.shape[1]
    by_e = w_out.reshape(CH, CH, pair).transpose(1, 0, 2)
    same = jnp.eye(GROUP, dtype=jnp.bool_)[None, :, None, :, None]
    full = jnp.where(same, by_e[:, None, :, None, :], jnp.zeros((), w_out.dtype))
    return full.reshape(CH * LANES, GROUP * pair)


def turned(right, perm):
    return lax.dot_general(perm, right, (((1,), (1,)), ((), ())), preferred_element_type=jnp.float32).astype(
        jnp.bfloat16
    )


def regroup(cols):
    res = cols // CH
    to = lax.broadcasted_iota(jnp.int32, (cols, cols), 0)
    source = lax.broadcasted_iota(jnp.int32, (cols, cols), 1)
    return jnp.where(source == (to % res) * CH + to // res, 1.0, 0.0).astype(jnp.bfloat16)


def early_kernel(places, *refs):
    nl = len(places)
    lefts = refs[:nl]
    own, beside, middle, opposite = refs[nl : nl + 4]
    sums = refs[nl + 4 : -4]
    late_ref, left_v, rt, sem = refs[-4:]
    l, r = lax.axis_index("left"), lax.axis_index("right")
    end = jnp.logical_or(l == 0, l == 3)
    rows = left_v.shape[0] // 3
    flip = 1 - 2 * (r % 2)
    far = (r + 2) % 4
    owners = (r, r + flip, far, far + flip)

    copies = []
    for n, (k, row) in enumerate(places):
        s = owners[k]
        odd = (s + l) % 2
        slot = jnp.where(s // 2 == l // 2, odd, 3 - odd)
        height = lefts[n].shape[0]
        at = pl.multiple_of(jnp.minimum(slot, 2) * rows + row, math.gcd(rows, row))
        late = late_ref.at[row : row + height, :]

        @pl.when(slot < 3)
        def _():
            pltpu.make_async_copy(lefts[n], left_v.at[pl.ds(at, height), :], sem.at[n]).start()

        @pl.when(slot == 3)
        def _():
            pltpu.make_async_copy(lefts[n], late, sem.at[n]).start()

        copies.append(pltpu.make_async_copy(lefts[n], late, sem.at[n]))

    first_row = 0
    for total in sums:
        cols = total.shape[0]
        perm = regroup(cols)
        here = pl.ds(first_row, cols)
        rt[here, :rows] = turned(own[:, here], perm)
        rt[here, rows : 2 * rows] = turned(beside[:, here], perm)

        @pl.when(end)
        def _():
            rt[here, 2 * rows :] = turned(opposite[:, here], perm)

        @pl.when(jnp.logical_not(end))
        def _():
            rt[here, 2 * rows :] = turned(middle[:, here], perm)

        first_row += cols
    for copy in copies:
        copy.wait()
    first_row = 0
    for total in sums:
        cols = total.shape[0]
        total[...] = jnp.dot(rt[first_row : first_row + cols, :], left_v[...], preferred_element_type=jnp.float32)
        first_row += cols


def early_sums(places, lefts, rights, cols):
    rows, width = lefts[0].shape
    vmem = pl.BlockSpec(memory_space=pltpu.VMEM)
    anywhere = pl.BlockSpec(memory_space=pl.ANY)
    parts = len(cols)
    out = pl.pallas_call(
        functools.partial(early_kernel, places),
        out_shape=[jax.ShapeDtypeStruct((c, width), jnp.float32) for c in cols]
        + [jax.ShapeDtypeStruct((rows, width), jnp.bfloat16)],
        in_specs=[anywhere] * len(lefts) + [vmem] * 4,
        out_specs=[vmem] * parts + [anywhere],
        scratch_shapes=[
            pltpu.VMEM((3 * rows, width), jnp.bfloat16),
            pltpu.VMEM((sum(cols), 3 * rows), jnp.bfloat16),
            pltpu.SemaphoreType.DMA((len(lefts),)),
        ],
        compiler_params=pltpu.CompilerParams(vmem_limit_bytes=EARLY_VMEM),
        cost_estimate=pl.CostEstimate(flops=1, bytes_accessed=1, transcendentals=0),
    )(*lefts, *rights)
    return out[:parts], out[parts]


def late_kernel(line, start, *refs):
    if line:
        sums, left, right, wide, counts = refs[:5]
    else:
        left, right, wide, counts = refs[:4]
    out_ref, rt, lhs, out_v, sem = refs[-5:]
    width = left.shape[1]
    res = right.shape[1] // CH
    rt[...] = turned(right[...], regroup(right.shape[1]))
    total = jnp.dot(rt[...], left[...], preferred_element_type=jnp.float32)
    if line:
        total += sums[...]
    outer = total.astype(jnp.bfloat16)
    for g in range(width // LANES):
        for e in range(CH):
            lhs[g * res : (g + 1) * res, e * LANES : (e + 1) * LANES] = outer[
                e * res : (e + 1) * res, g * LANES : (g + 1) * LANES
            ]
    projected = jnp.dot(lhs[...], wide[...], preferred_element_type=jnp.float32)
    pair = out_v.shape[2]
    for g in range(width // LANES):
        for i in range(GROUP):
            row = g * GROUP + i
            out_v[row] = projected[g * res : (g + 1) * res, i * pair : (i + 1) * pair] / counts[:, row : row + 1]
    out_copy = pltpu.make_async_copy(out_v, out_ref.at[:, pl.ds(start, res), :], sem)
    out_copy.start()
    out_copy.wait()


def pair_features(line, start, operands, counts, right_dev, before):
    vmem = pl.BlockSpec(memory_space=pltpu.VMEM)
    anywhere = pl.BlockSpec(memory_space=pl.ANY)
    left, right, wide = operands[-3:]
    rows, width = left.shape
    cols = right.shape[1]
    res, left_dev = cols // CH, width // CH
    pair = wide.shape[1] // GROUP
    operands = [*operands, counts]
    specs = [vmem] * len(operands)
    aliases = {}
    if before is not None:
        aliases = {len(operands): 0}
        operands.append(before)
        specs.append(anywhere)
    return pl.pallas_call(
        functools.partial(late_kernel, line, start),
        out_shape=jax.ShapeDtypeStruct((left_dev, right_dev, pair), jnp.float32),
        in_specs=specs,
        out_specs=anywhere,
        input_output_aliases=aliases,
        scratch_shapes=[
            pltpu.VMEM((cols, rows), jnp.bfloat16),
            pltpu.VMEM((width // LANES * res, CH * LANES), jnp.bfloat16),
            pltpu.VMEM((left_dev, res, pair), jnp.float32),
            pltpu.SemaphoreType.DMA,
        ],
        compiler_params=pltpu.CompilerParams(vmem_limit_bytes=LATE_VMEM if line else 2 * LATE_VMEM),
        cost_estimate=pl.CostEstimate(flops=1, bytes_accessed=1, transcendentals=0),
    )(*operands)


def gather_line(left_act, right_act, wide):
    cut = right_act.shape[1] * FIRST_PART // PART_UNITS
    end = lax.axis_index("left") % 3 == 0

    def hop(x, pairs):
        return lax.ppermute(x, "left", pairs)

    def partner(x, step):
        return lax.ppermute(x, "right", [(i, i ^ step) for i in range(4)])

    def last(cols, *arrived):
        inward = end
        for x in arrived:
            same = x[: right_act.shape[0], : cut]
            inward = jnp.logical_and(inward, same == same)
        return hop(jnp.where(inward, right_act[:, cols], middle[:, cols]), ((0, 2), (3, 1), (1, 0), (2, 3)))

    far = partner(left_act, CORES)
    near = partner(left_act, 1)
    beside = hop(right_act, [(i, i ^ 1) for i in range(4)])
    middle = hop(right_act, ((1, 2), (2, 1)))
    opposite = hop(right_act, ((0, 3), (3, 0)))
    late = (last(slice(0, cut), beside), last(slice(cut, None), wide))
    unit = far.shape[0] // sum(CROSS_PARTS)
    starts = [sum(CROSS_PARTS[:n]) * unit for n in range(len(CROSS_PARTS))]
    cross = [partner(far[n : n + h * unit], 1) for n, h in zip(starts, CROSS_PARTS)]
    lefts = [left_act, near, far, *cross]
    places = [(0, 0), (1, 0), (2, 0)] + [(3, n) for n in starts]
    return places, lefts, (right_act, beside, middle, opposite), late


def shards(line, left_act, right_act, counts, w_out):
    right_dev = counts.shape[1]
    cut = right_dev * FIRST_PART // PART_UNITS
    by_right = counts.astype(jnp.float32).T
    count_parts = (by_right[:cut], by_right[cut:])
    wide = spread_weights(w_out)
    if line:
        places, lefts, early, late = gather_line(left_act, right_act, wide)
        sums, left_late = early_sums(places, lefts, early, [x.shape[1] for x in late])
        operands = [(sums[p], left_late, late[p], wide) for p in range(2)]
    else:
        left_full = lax.all_gather(left_act, "right", axis=0, tiled=True)
        full = lax.all_gather(right_act, "left", axis=0, tiled=True)
        operands = [(left_full, x, wide) for x in (full[:, : cut * CH], full[:, cut * CH :])]
    out = None
    for start, given, count in zip((0, cut), operands, count_parts):
        out = pair_features(line, start, given, count, right_dev, out)
    return out


def solution(mesh):
    in_specs = (
        P(("groups", "right"), "left"),
        P(("groups", "left"), "right"),
        P(("groups", "left"), "right"),
        P(),
    )
    out_specs = P(("groups", "left"), "right", None)
    line = mesh.shape["left"] == 4 and mesh.shape["right"] == 4
    body = functools.partial(shards, line)
    return jax.shard_map(body, mesh=mesh, in_specs=in_specs, out_specs=out_specs, check_vma=False)
```
